32 devices in a mesh: seq: 8 (over z, x), feat: 4 (over y, core).
Axes of the slice: x: 2, y: 2, z: 4, core: 2. Of those that a mesh axis runs over, the one named last changes fastest.
Arguments:
- tokens: bfloat16 [4096, 8192], P('seq', 'feat'), may hold values from -6 to 6
- butterfly: bfloat16 [16, 5, 512, 896], P('feat'), may hold values from -0.125 to 0.125
- low_in: bfloat16 [8192, 256], P('feat'), may hold values from -0.0625 to 0.0625
- low_out: bfloat16 [256, 14336], P(None, 'feat'), may hold values from -0.375 to 0.375
- cotangent: bfloat16 [4096, 14336], P('seq', 'feat'), may hold values from -6 to 6
Outputs:
- activated: bfloat16 [4096, 14336], P('seq', 'feat')
- tokens_grad: bfloat16 [4096, 8192], P('seq', 'feat')
- butterfly_grad: float32 [16, 5, 512, 896], P('feat', None, 'seq')
- low_in_grad: float32 [8192, 256], P('feat', 'seq')
- low_out_grad: float32 [256, 14336], P('seq', 'feat')
The draws below stay inside these ranges and needn't reach their ends.
All inputs are finite; a program needn't handle non-finite values.
Results may differ from the reference program's by a relative error of at most 0.0058.
Values may be sent and summed in bfloat16 or wider, within the bound.
A program may use at most 192 MiB of HBM per device.

```python
import jax
import jax.numpy as jnp

BLOCKS = 16
BLOCK_WIDTH = 512
HIDDEN_BLOCK = 896
RANK = 256
MODEL_WIDTH = 8192
HIDDEN_SIZE = 14336
TOKENS = 4096


def steps_of(key, dims, shards, smallest, high):
    gain = 1.0
    for axis_at, blocks in shards:
        heights = jax.random.uniform(jax.random.fold_in(jax.random.fold_in(key, 6), axis_at), (blocks,), jnp.float32, smallest / len(shards), high / len(shards))
        gain = gain * jnp.repeat(jnp.exp(heights), dims[axis_at] // blocks).reshape((-1,) + (1,) * (len(dims) - 1 - axis_at))
    return gain


def centred(stream_key, shape, width, limit, split=(), dtype=jnp.bfloat16):
    factor_of = steps_of(stream_key, shape, split, -0.22, 0.18) if split else 1.0
    array = jax.random.normal(stream_key, shape, jnp.float32) * width * factor_of
    return jnp.minimum(jnp.maximum(array, -limit), limit).astype(dtype)


def setup_inputs(seed: int = 0) -> dict:
    arg_keys = jax.random.split(jax.random.key(seed), 6)
    return {
        "tokens": centred(arg_keys[0], (TOKENS, MODEL_WIDTH), 1.0, 6.0, ((0, 8), (1, 4))),
        "butterfly": centred(arg_keys[1], (BLOCKS, 5, BLOCK_WIDTH, HIDDEN_BLOCK), (5 * BLOCK_WIDTH) ** -0.5, 0.125, ((0, 4),)),
        "low_in": centred(arg_keys[2], (MODEL_WIDTH, RANK), MODEL_WIDTH ** -0.5, 0.0625, ((0, 4),)),
        "low_out": centred(arg_keys[3], (RANK, HIDDEN_SIZE), RANK ** -0.5, 0.375, ((1, 4),)),
        "cotangent": centred(arg_keys[4], (TOKENS, HIDDEN_SIZE), 1.0, 6.0, ((0, 8), (1, 4))),
    }


def gelu_tanh(values):
    return jax.nn.gelu(values, approximate=True)

def source_block(target, slot):
    if slot == 0:
        return target
    return target ^ 1 << slot - 1

def reference(tokens, butterfly, low_in, low_out, cotangent):
    blocks = tokens.reshape(TOKENS, BLOCKS, BLOCK_WIDTH)
    low_rank = jnp.dot(tokens, low_in, preferred_element_type=jnp.float32).astype(jnp.bfloat16)
    columns = []
    for target in range(BLOCKS):
        upper = low_out[:, target * HIDDEN_BLOCK:(target + 1) * HIDDEN_BLOCK]
        total = jnp.dot(low_rank, upper, preferred_element_type=jnp.float32)
        for slot in range(5):
            total = total + jnp.dot(blocks[:, source_block(target, slot)], butterfly[target, slot], preferred_element_type=jnp.float32)
        columns.append(total)
    pre = jnp.concatenate(columns, axis=1)
    activ, pullback = jax.vjp(gelu_tanh, pre)
    activated = activ.astype(jnp.bfloat16)
    grad_pre = pullback(cotangent.astype(jnp.float32))[0].astype(jnp.bfloat16)
    low_grad = jnp.dot(grad_pre, low_out.T, preferred_element_type=jnp.float32).astype(jnp.bfloat16)
    grad_blocks = grad_pre.reshape(TOKENS, BLOCKS, HIDDEN_BLOCK)
    pieces = []
    for source in range(BLOCKS):
        rows_in = low_in[source * BLOCK_WIDTH:(source + 1) * BLOCK_WIDTH]
        total = jnp.dot(low_grad, rows_in.T, preferred_element_type=jnp.float32)
        total = total + jnp.dot(grad_blocks[:, source], butterfly[source, 0].T, preferred_element_type=jnp.float32)
        for bit_level in range(4):
            target = source ^ 1 << bit_level
            total = total + jnp.dot(grad_blocks[:, target], butterfly[target, 1 + bit_level].T, preferred_element_type=jnp.float32)
        pieces.append(total)
    tokens_grad = jnp.concatenate(pieces, axis=1).astype(jnp.bfloat16)
    grads = []
    for target in range(BLOCKS):
        row_list = []
        for slot in range(5):
            row_list.append(jnp.dot(blocks[:, source_block(target, slot)].T, grad_blocks[:, target], preferred_element_type=jnp.float32))
        grads.append(jnp.stack(row_list, axis=0))
    butterfly_grad = jnp.stack(grads, axis=0)
    low_in_grad = jnp.dot(tokens.T, low_grad, preferred_element_type=jnp.float32)
    low_out_grad = jnp.dot(low_rank.T, grad_pre, preferred_element_type=jnp.float32)
    return (activated, tokens_grad, butterfly_grad, low_in_grad, low_out_grad)
```

```python
import functools

import jax
import jax.numpy as jnp
from jax import lax
from jax.experimental import pallas as pl
from jax.experimental.pallas import tpu as pltpu
from jax.sharding import PartitionSpec as P

F32 = jnp.float32
BF16 = jnp.bfloat16


def swap(block, axis, distance):
    count = lax.axis_size(axis)
    return lax.ppermute(block, axis, [(i, i ^ distance) for i in range(count)])


def sum_over(part, axis):
    distance = 1
    while distance < lax.axis_size(axis):
        part = part + swap(part, axis, distance)
        distance *= 2
    return part


def line_scatter(parts, place, count):
    def pick(at):
        return lax.dynamic_index_in_dim(parts, jnp.clip(at, 0, count - 1), 0, keepdims=False)

    total = pick(place).astype(F32)
    for way in (1, -1):
        moving = None
        for step in range(1, count):
            term = pick(place + way * (count - step))
            if moving is not None:
                term = (term.astype(F32) + moving.astype(F32)).astype(BF16)
            froms = range(step) if way == 1 else range(count - step, count)
            route = [(2 * z + x, 2 * (z + way) + x) for z in froms for x in range(2)]
            moving = lax.ppermute(term, "seq", route)
        if moving is not None:
            total = total + moving.astype(F32)
    return total


def forward_body(slots, tile, *refs):
    sources = refs[:slots]
    low_rank, weights, low_out, cotangent, activated, grad_pre = refs[slots:]
    gain = 0.7978845608028654
    rows = low_rank.shape[0]
    for top in range(0, rows, tile):
        at = pl.ds(top, tile)
        value = jnp.dot(low_rank[at, :], low_out[...], preferred_element_type=F32)
        for slot in range(slots):
            value += jnp.dot(sources[slot][at, :], weights[0, slot], preferred_element_type=F32)
        square = value * value
        bend = jnp.tanh(gain * value * (1.0 + 0.044715 * square))
        half = 0.5 * (1.0 + bend)
        activated[at, :] = (value * half).astype(BF16)
        slope = half + 0.5 * gain * value * (1.0 - bend * bend) * (1.0 + 3 * 0.044715 * square)
        grad_pre[0, at, :] = (cotangent[at, :].astype(F32) * slope).astype(BF16)


def forward(tokens, partners, low_rank, butterfly, low_out, cotangent):
    rows = tokens.shape[0]
    per_dev, slots, block, hidden = butterfly.shape
    rank = low_out.shape[0]
    local_bits = per_dev.bit_length() - 1
    tile = 256 if rows % 256 == 0 else rows

    def column(distance):
        return pl.BlockSpec((rows, block), lambda k: (0, k ^ distance))

    arrays = [tokens] * (1 + local_bits) + partners
    specs = [column(0)] + [column(1 << b) for b in range(local_bits)] + [column(0)] * len(partners)
    wide = pl.BlockSpec((rows, hidden), lambda k: (0, k))
    return pl.pallas_call(
        functools.partial(forward_body, slots, tile),
        grid=(per_dev,),
        in_specs=specs
        + [
            pl.BlockSpec((rows, rank), lambda k: (0, 0)),
            pl.BlockSpec((1, slots, block, hidden), lambda k: (k, 0, 0, 0)),
            pl.BlockSpec((rank, hidden), lambda k: (0, k)),
            wide,
        ],
        out_specs=[wide, pl.BlockSpec((1, rows, hidden), lambda k: (k, 0, 0))],
        out_shape=[
            jax.ShapeDtypeStruct((rows, per_dev * hidden), BF16),
            jax.ShapeDtypeStruct((per_dev, rows, hidden), BF16),
        ],
        compiler_params=pltpu.CompilerParams(vmem_limit_bytes=48 << 20),
        cost_estimate=pl.CostEstimate(
            flops=2 * rows * per_dev * hidden * (slots * block + rank),
            bytes_accessed=2 * (butterfly.size + 3 * cotangent.size + slots * tokens.size),
            transcendentals=cotangent.size,
        ),
    )(*arrays, low_rank, butterfly, low_out, cotangent)


def dot_t(left, right):
    return lax.dot_general(left, right, (((1,), (1,)), ((), ())), preferred_element_type=F32)


def local(tokens, butterfly, low_in, low_out, cotangent):
    rows = tokens.shape[0]
    per_dev, slots, block, hidden = butterfly.shape
    rank = low_out.shape[0]
    seq = lax.axis_size("seq")
    feat = lax.axis_size("feat")
    local_bits = per_dev.bit_length() - 1
    remote = slots - 1 - local_bits
    pairs = seq // 2
    me = lax.axis_index("seq")
    side = me % 2
    place = me // 2
    width = block // seq
    low_width = rank // seq

    low_rank = sum_over(jnp.dot(tokens, low_in, preferred_element_type=F32), "feat").astype(BF16)
    partners = [swap(tokens, "feat", 1 << r) for r in range(remote)]

    def halves(wide, parts):
        return wide.T.reshape(parts, pairs, 2, -1, rows)

    def side_of(array, which):
        return lax.dynamic_index_in_dim(array, which, 2, keepdims=False)

    own_t = halves(tokens, per_dev)
    far_own = swap(side_of(own_t, 1 - side), "seq", 1)
    far = [far_own] + [swap(far_own, "feat", 1 << r) for r in range(remote)]
    near = [side_of(own_t, side)] + [side_of(halves(p, per_dev), side) for p in partners]
    both = [jnp.concatenate([n, f], axis=-1) for n, f in zip(near, far)]
    rank_t = halves(low_rank, 1)
    both_rank = jnp.concatenate(
        [side_of(rank_t, side), swap(side_of(rank_t, 1 - side), "seq", 1)], axis=-1
    )[0]

    activated, grad_pre = forward(tokens, partners, low_rank, butterfly, low_out, cotangent)

    weight_rows = []
    for k in range(per_dev):
        grads = jnp.concatenate([grad_pre[k], swap(grad_pre[k], "seq", 1)], axis=0)
        picks = [both[0][k]] + [both[0][k ^ 1 << b] for b in range(local_bits)]
        picks += [both[1 + r][k] for r in range(remote)]
        left = jnp.concatenate(picks + [both_rank], axis=1)
        deep = left.shape[1]
        terms = jnp.dot(
            left.reshape(pairs * deep, 2 * rows), grads, preferred_element_type=F32
        ).astype(BF16)
        weight_rows.append(line_scatter(terms.reshape(pairs, deep, hidden), place, pairs))
    butterfly_grad = jnp.stack(
        [w[: slots * width].reshape(slots, width, hidden) for w in weight_rows], axis=0
    )
    low_out_grad = jnp.concatenate([w[slots * width :] for w in weight_rows], axis=1)

    low_back = sum(
        dot_t(grad_pre[k], low_out[:, k * hidden : (k + 1) * hidden]) for k in range(per_dev)
    )
    low_grad = sum_over(low_back, "feat").astype(BF16)
    in_terms = lax.dot_general(
        low_grad, tokens, (((0,), (0,)), ((), ())), preferred_element_type=F32
    ).reshape(pairs, 2, low_width, per_dev * block)
    in_own = lax.dynamic_index_in_dim(in_terms, side, 1, keepdims=False)
    in_far = lax.dynamic_index_in_dim(in_terms, 1 - side, 1, keepdims=False).astype(BF16)
    in_pair = (in_own + swap(in_far, "seq", 1).astype(F32)).astype(BF16)
    low_in_grad = line_scatter(in_pair, place, pairs).T

    came = []
    for r in range(remote):
        slot = 1 + local_bits + r
        partial = [dot_t(grad_pre[k], butterfly[k, slot]).astype(BF16) for k in range(per_dev)]
        came.append(swap(jnp.concatenate(partial, axis=1), "feat", 1 << r))
    pieces = []
    for j in range(per_dev):
        at = slice(j * block, (j + 1) * block)
        total = dot_t(low_grad, low_in[at]) + dot_t(grad_pre[j], butterfly[j, 0])
        for b in range(local_bits):
            i = j ^ 1 << b
            total = total + dot_t(grad_pre[i], butterfly[i, 1 + b])
        for c in came:
            total = total + c[:, at].astype(F32)
        pieces.append(total.astype(BF16))
    tokens_grad = jnp.concatenate(pieces, axis=1)
    return (activated, tokens_grad, butterfly_grad, low_in_grad, low_out_grad)


def solution(mesh):
    placed = (
        P("seq", "feat"),
        P("feat", None, None, None),
        P("feat", None),
        P(None, "feat"),
        P("seq", "feat"),
    )
    return jax.shard_map(
        local,
        mesh=mesh,
        in_specs=placed,
        out_specs=(
            P("seq", "feat"),
            P("seq", "feat"),
            P("feat", None, "seq", None),
            P("feat", "seq"),
            P("seq", "feat"),
        ),
        check_vma=False,
    )
```

```python
import functools

import jax
import jax.numpy as jnp
from jax import lax
from jax.experimental import pallas as pl
from jax.experimental.pallas import tpu as pltpu
from jax.sharding import PartitionSpec as P

F32 = jnp.float32
BF16 = jnp.bfloat16


def swap(block, axis, distance):
    count = lax.axis_size(axis)
    return lax.ppermute(block, axis, [(i, i ^ distance) for i in range(count)])


def sum_over(part, axis):
    distance = lax.axis_size(axis) // 2
    while distance > 0:
        part = part + swap(part, axis, distance)
        distance //= 2
    return part


def line_scatter(parts, place, count):
    def pick(at):
        return lax.dynamic_index_in_dim(parts, jnp.clip(at, 0, count - 1), 0, keepdims=False)

    total = pick(place).astype(F32)
    firsts = []
    for way in (1, -1):
        moving = None
        for step in range(1, count):
            term = pick(place + way * (count - step))
            if moving is not None:
                term = (term.astype(F32) + moving.astype(F32)).astype(BF16)
            froms = range(step) if way == 1 else range(count - step, count)
            route = [(2 * z + x, 2 * (z + way) + x) for z in froms for x in range(2)]
            moving = lax.ppermute(term, "seq", route)
            if step == 1:
                firsts.append(moving)
        if moving is not None:
            total = total + moving.astype(F32)
    return total, firsts


def forward_body(slots, *refs):
    sources = refs[:slots]
    low_rank, weights, low_out, cotangent = refs[slots : slots + 4]
    activated, grad_pre = refs[-2:]
    gain = 0.7978845608028654
    value = jnp.dot(low_rank[...], low_out[...], preferred_element_type=F32)
    for slot in range(slots):
        value += jnp.dot(sources[slot][...], weights[0, slot], preferred_element_type=F32)
    square = value * value
    bend = jnp.tanh(gain * value * (1.0 + 0.044715 * square))
    half = 0.5 * (1.0 + bend)
    activated[...] = (value * half).astype(BF16)
    slope = half + 0.5 * gain * value * (1.0 - bend * bend) * (1.0 + 3 * 0.044715 * square)
    grad_pre[...] = (cotangent[...].astype(F32) * slope).astype(BF16)


def forward(k, tokens, partners, low_rank, butterfly, low_out, cotangent, activated):
    rows = tokens.shape[0]
    per_dev, slots, block, hidden = butterfly.shape
    rank = low_out.shape[0]
    local_bits = per_dev.bit_length() - 1
    tile = 256 if rows % 256 == 0 else rows

    def column(at):
        return pl.BlockSpec((tile, block), lambda t: (t, at))

    arrays = [tokens] * (1 + local_bits) + partners
    specs = [column(k)] + [column(k ^ 1 << b) for b in range(local_bits)]
    specs += [column(0)] * len(partners)
    wide = pl.BlockSpec((tile, hidden), lambda t: (t, k))
    arrays += [low_rank, butterfly, low_out, cotangent]
    specs += [
        pl.BlockSpec((tile, rank), lambda t: (t, 0)),
        pl.BlockSpec((1, slots, block, hidden), lambda t: (k, 0, 0, 0)),
        pl.BlockSpec((rank, hidden), lambda t: (0, k)),
        wide,
    ]
    aliases = {}
    if activated is not None:
        aliases = {len(arrays): 0}
        arrays.append(activated)
        specs.append(pl.BlockSpec(memory_space=pl.ANY))
    return pl.pallas_call(
        functools.partial(forward_body, slots),
        grid=(rows // tile,),
        in_specs=specs,
        out_specs=[wide, pl.BlockSpec((tile, hidden), lambda t: (t, 0))],
        out_shape=[
            jax.ShapeDtypeStruct((rows, per_dev * hidden), BF16),
            jax.ShapeDtypeStruct((rows, hidden), BF16),
        ],
        input_output_aliases=aliases,
        compiler_params=pltpu.CompilerParams(vmem_limit_bytes=40 << 20),
        cost_estimate=pl.CostEstimate(
            flops=2 * rows * hidden * (slots * block + rank),
            bytes_accessed=2 * (slots * block * hidden + 3 * rows * hidden + slots * rows * block),
            transcendentals=rows * hidden,
        ),
    )(*arrays)


def dot_t(left, right):
    return lax.dot_general(left, right, (((1,), (1,)), ((), ())), preferred_element_type=F32)


def after(value, *earlier):
    return lax.optimization_barrier((value,) + earlier)[0]


def local(tokens, butterfly, low_in, low_out, cotangent):
    rows = tokens.shape[0]
    per_dev, slots, block, hidden = butterfly.shape
    rank = low_out.shape[0]
    seq = lax.axis_size("seq")
    local_bits = per_dev.bit_length() - 1
    remote = slots - 1 - local_bits
    pairs = seq // 2
    me = lax.axis_index("seq")
    side = me % 2
    place = me // 2
    width = block // seq
    low_width = rank // seq

    def halves(wide):
        return wide.T.reshape(pairs, 2, -1, rows)

    def side_of(array, which, axis=1):
        return lax.dynamic_index_in_dim(array, which, axis, keepdims=False)

    def columns(k):
        return slice(k * block, (k + 1) * block)

    low_part = jnp.dot(tokens, low_in, preferred_element_type=F32)
    low_rank = sum_over(low_part, "feat").astype(BF16)
    tokens_late = after(tokens, low_part)
    own_t = tokens_late.T.reshape(per_dev, pairs, 2, width, rows)
    near = [side_of(own_t, side, 2)] + [[] for _ in range(remote)]
    far = [[] for _ in range(1 + remote)]
    away = side_of(own_t, 1 - side, 2)
    partners = [[] for _ in range(remote)]
    activated = None
    grad_pre = []
    grads = []
    for k in range(per_dev):
        chunk = tokens_late[:, columns(k)]
        if k > 0:
            chunk = after(chunk, low_rank, far[0][k - 1])
        if k > 1:
            chunk = after(chunk, grad_pre[k - 2])
        far[0].append(swap(away[k], "seq", 1))
        for r in reversed(range(remote)):
            partners[r].append(swap(chunk, "feat", 1 << r))
            far[1 + r].append(swap(far[0][k], "feat", 1 << r))
        activated, one = forward(
            k, tokens, [p[k] for p in partners], low_rank, butterfly, low_out, cotangent, activated
        )
        grad_pre.append(one)
        grads.append(jnp.concatenate([one, swap(one, "seq", 1)], axis=0))
        for r in range(remote):
            near[1 + r].append(side_of(halves(partners[r][k]), side))
    rank_t = halves(low_rank)
    both_rank = jnp.concatenate(
        [side_of(rank_t, side), swap(side_of(rank_t, 1 - side), "seq", 1)], axis=-1
    )

    weight_rows = []
    late = []
    for k in range(per_dev):
        sources = [(0, k)] + [(0, k ^ 1 << b) for b in range(local_bits)]
        sources += [(1 + r, k) for r in range(remote)]
        picks = [jnp.concatenate([near[a][b], far[a][b]], axis=-1) for a, b in sources]
        left = jnp.concatenate(picks + [both_rank], axis=1)
        deep = left.shape[1]
        terms = jnp.dot(
            left.reshape(pairs * deep, 2 * rows), grads[k], preferred_element_type=F32
        ).astype(BF16)
        sums, firsts = line_scatter(terms.reshape(pairs, deep, hidden), place, pairs)
        weight_rows.append(sums)
        late.append(after(grad_pre[k], terms, *firsts))
    butterfly_grad = jnp.stack(
        [w[: slots * width].reshape(slots, width, hidden) for w in weight_rows], axis=0
    )
    low_out_grad = jnp.concatenate([w[slots * width :] for w in weight_rows], axis=1)

    low_back = sum(
        dot_t(late[k], low_out[:, k * hidden : (k + 1) * hidden]) for k in range(per_dev)
    )
    low_grad = sum_over(low_back, "feat").astype(BF16)
    in_terms = lax.dot_general(
        low_grad, tokens, (((0,), (0,)), ((), ())), preferred_element_type=F32
    ).reshape(pairs, 2, low_width, per_dev * block)
    in_far = side_of(in_terms, 1 - side).astype(BF16)
    in_pair = (side_of(in_terms, side) + swap(in_far, "seq", 1).astype(F32)).astype(BF16)
    low_in_grad = line_scatter(in_pair, place, pairs)[0].T

    came = [[] for _ in range(remote)]
    for k in range(per_dev):
        for r in reversed(range(remote)):
            partial = dot_t(late[k], butterfly[k, 1 + local_bits + r]).astype(BF16)
            came[r].append(swap(partial, "feat", 1 << r))
    pieces = []
    for j in range(per_dev):
        total = dot_t(low_grad, low_in[columns(j)]) + dot_t(late[j], butterfly[j, 0])
        for b in range(local_bits):
            i = j ^ 1 << b
            total = total + dot_t(late[i], butterfly[i, 1 + b])
        for c in came:
            total = total + c[j].astype(F32)
        pieces.append(total.astype(BF16))
    tokens_grad = jnp.concatenate(pieces, axis=1)
    return (activated, tokens_grad, butterfly_grad, low_in_grad, low_out_grad)


def solution(mesh):
    placed = (
        P("seq", "feat"),
        P("feat", None, None, None),
        P("feat", None),
        P(None, "feat"),
        P("seq", "feat"),
    )
    return jax.shard_map(
        local,
        mesh=mesh,
        in_specs=placed,
        out_specs=(
            P("seq", "feat"),
            P("seq", "feat"),
            P("feat", None, "seq", None),
            P("feat", "seq"),
            P("seq", "feat"),
        ),
        check_vma=False,
    )
```

```python
import functools

import jax
import jax.numpy as jnp
from jax import lax
from jax.experimental import pallas as pl
from jax.experimental.pallas import tpu as pltpu
from jax.sharding import PartitionSpec as P

F32 = jnp.float32
BF16 = jnp.bfloat16


def swap(block, axis, distance):
    count = lax.axis_size(axis)
    return lax.ppermute(block, axis, [(i, i ^ distance) for i in range(count)])


def sum_over(part, axis):
    distance = lax.axis_size(axis) // 2
    first = None
    while distance > 0:
        part = part + swap(part, axis, distance)
        first = part if first is None else first
        distance //= 2
    return part, first


def after(value, *earlier):
    return lax.optimization_barrier((value,) + earlier)[0]


def line_scatter(parts, place, count):
    def pick(at):
        return lax.dynamic_index_in_dim(parts, jnp.clip(at, 0, count - 1), 0, keepdims=False)

    total = pick(place).astype(F32)
    firsts = []
    for way in (1, -1):
        moving = None
        for step in range(1, count):
            term = pick(place + way * (count - step))
            if moving is not None:
                term = (term.astype(F32) + moving.astype(F32)).astype(BF16)
            froms = range(step) if way == 1 else range(count - step, count)
            route = [(2 * z + x, 2 * (z + way) + x) for z in froms for x in range(2)]
            moving = lax.ppermute(term, "seq", route)
            if step == 1:
                firsts.append(moving)
        if moving is not None:
            total = total + moving.astype(F32)
    return total, firsts


def forward_body(slots, tile, *refs):
    sources = refs[:slots]
    low_rank, weights, low_out, cotangent, activated, grad_pre = refs[slots:]
    gain = 0.7978845608028654
    rows = low_rank.shape[0]
    for top in range(0, rows, tile):
        at = pl.ds(top, tile)
        value = jnp.dot(low_rank[at, :], low_out[...], preferred_element_type=F32)
        for slot in range(slots):
            value += jnp.dot(sources[slot][at, :], weights[0, slot], preferred_element_type=F32)
        square = value * value
        bend = jnp.tanh(gain * value * (1.0 + 0.044715 * square))
        half = 0.5 * (1.0 + bend)
        activated[at, :] = (value * half).astype(BF16)
        slope = half + 0.5 * gain * value * (1.0 - bend * bend) * (1.0 + 3 * 0.044715 * square)
        grad_pre[0, at, :] = (cotangent[at, :].astype(F32) * slope).astype(BF16)


def forward(tokens, partners, low_rank, butterfly, low_out, cotangent):
    rows = tokens.shape[0]
    per_dev, slots, block, hidden = butterfly.shape
    rank = low_out.shape[0]
    local_bits = per_dev.bit_length() - 1
    tile = 256 if rows % 256 == 0 else rows

    def column(distance):
        return pl.BlockSpec((rows, block), lambda k: (0, k ^ distance))

    arrays = [tokens] * (1 + local_bits) + partners
    specs = [column(0)] + [column(1 << b) for b in range(local_bits)] + [column(0)] * len(partners)
    wide = pl.BlockSpec((rows, hidden), lambda k: (0, k))
    return pl.pallas_call(
        functools.partial(forward_body, slots, tile),
        grid=(per_dev,),
        in_specs=specs
        + [
            pl.BlockSpec((rows, rank), lambda k: (0, 0)),
            pl.BlockSpec((1, slots, block, hidden), lambda k: (k, 0, 0, 0)),
            pl.BlockSpec((rank, hidden), lambda k: (0, k)),
            wide,
        ],
        out_specs=[wide, pl.BlockSpec((1, rows, hidden), lambda k: (k, 0, 0))],
        out_shape=[
            jax.ShapeDtypeStruct((rows, per_dev * hidden), BF16),
            jax.ShapeDtypeStruct((per_dev, rows, hidden), BF16),
        ],
        compiler_params=pltpu.CompilerParams(vmem_limit_bytes=48 << 20),
        cost_estimate=pl.CostEstimate(
            flops=2 * rows * per_dev * hidden * (slots * block + rank),
            bytes_accessed=2 * (butterfly.size + 3 * cotangent.size + slots * tokens.size),
            transcendentals=cotangent.size,
        ),
    )(*arrays, low_rank, butterfly, low_out, cotangent)


def dot_t(left, right):
    return lax.dot_general(left, right, (((1,), (1,)), ((), ())), preferred_element_type=F32)


def local(tokens, butterfly, low_in, low_out, cotangent):
    rows = tokens.shape[0]
    per_dev, slots, block, hidden = butterfly.shape
    seq = lax.axis_size("seq")
    feat = lax.axis_size("feat")
    local_bits = per_dev.bit_length() - 1
    remote = slots - 1 - local_bits
    pairs = seq // 2
    me = lax.axis_index("seq")
    side = me % 2
    place = me // 2
    width = block // seq

    low_rank, first = sum_over(jnp.dot(tokens, low_in, preferred_element_type=F32), "feat")
    low_rank = low_rank.astype(BF16)
    leaving = after(tokens, first)
    partners = [swap(leaving, "feat", 1 << r) for r in reversed(range(remote))][::-1]

    def halves(wide, parts):
        return wide.T.reshape(parts, pairs, 2, -1, rows)

    def side_of(array, which):
        return lax.dynamic_index_in_dim(array, which, 2, keepdims=False)

    own_t = halves(tokens, per_dev)
    far_own = swap(side_of(own_t, 1 - side), "seq", 1)
    far = [far_own] + [swap(far_own, "feat", 1 << r) for r in range(remote)]
    activated, grad_pre = forward(tokens, partners, low_rank, butterfly, low_out, cotangent)
    grads = []
    for k in range(per_dev):
        grads.append(jnp.concatenate([grad_pre[k], swap(grad_pre[k], "seq", 1)], axis=0))

    near = [side_of(own_t, side)]
    near += [side_of(halves(after(p, grad_pre), per_dev), side) for p in partners]
    both = [jnp.concatenate([n, f], axis=-1) for n, f in zip(near, far)]
    rank_t = halves(low_rank, 1)
    both_rank = jnp.concatenate(
        [side_of(rank_t, side), swap(side_of(rank_t, 1 - side), "seq", 1)], axis=-1
    )[0]

    sums = []
    late = []
    group = max(1, per_dev // 2)
    for head in range(0, per_dev, group):
        terms = []
        for k in range(head, head + group):
            picks = [both[0][k]] + [both[0][k ^ 1 << b] for b in range(local_bits)]
            picks += [both[1 + r][k] for r in range(remote)]
            left = jnp.concatenate(picks + [both_rank], axis=1)
            deep = left.shape[1]
            term = jnp.dot(
                left.reshape(pairs * deep, 2 * rows), grads[k], preferred_element_type=F32
            ).astype(BF16)
            terms.append(term.reshape(pairs, deep, hidden))
        total, firsts = line_scatter(jnp.stack(terms, axis=1), place, pairs)
        late += [after(grad_pre[k], *terms, *firsts) for k in range(head, head + group)]
        sums.append(total)
    weight_rows = [w[k] for w in sums for k in range(group)]
    butterfly_grad = jnp.concatenate(
        [w[:, : slots * width].reshape(group, slots, width, hidden) for w in sums], axis=0
    )
    low_out_grad = jnp.concatenate([w[slots * width :] for w in weight_rows], axis=1)

    low_back = sum(
        dot_t(late[k], low_out[:, k * hidden : (k + 1) * hidden]) for k in range(per_dev)
    )
    low_grad = sum_over(low_back, "feat")[0].astype(BF16)
    in_terms = lax.dot_general(
        low_grad, tokens, (((0,), (0,)), ((), ())), preferred_element_type=F32
    )
    low_in_grad = lax.psum_scatter(in_terms, "seq", scatter_dimension=0, tiled=True).T

    came = []
    for r in range(remote):
        slot = 1 + local_bits + r
        partial = [dot_t(late[k], butterfly[k, slot]).astype(BF16) for k in range(per_dev)]
        came.append(swap(jnp.concatenate(partial, axis=1), "feat", 1 << r))
    pieces = []
    for j in range(per_dev):
        at = slice(j * block, (j + 1) * block)
        total = dot_t(low_grad, low_in[at]) + dot_t(late[j], butterfly[j, 0])
        for b in range(local_bits):
            i = j ^ 1 << b
            total = total + dot_t(late[i], butterfly[i, 1 + b])
        for c in came:
            total = total + c[:, at].astype(F32)
        pieces.append(total.astype(BF16))
    tokens_grad = jnp.concatenate(pieces, axis=1)
    return (activated, tokens_grad, butterfly_grad, low_in_grad, low_out_grad)


def solution(mesh):
    placed = (
        P("seq", "feat"),
        P("feat", None, None, None),
        P("feat", None),
        P(None, "feat"),
        P("seq", "feat"),
    )
    return jax.shard_map(
        local,
        mesh=mesh,
        in_specs=placed,
        out_specs=(
            P("seq", "feat"),
            P("seq", "feat"),
            P("feat", None, "seq", None),
            P("feat", "seq"),
            P("seq", "feat"),
        ),
        check_vma=False,
    )
```
